32 devices in a mesh: band: 4 (over x, core), isdf: 8 (over z, y).
Axes of the slice: x: 2, y: 2, z: 4, core: 2. Of those that a mesh axis runs over, the one named last changes fastest.
Arguments:
- trial: bfloat16 [512, 2, 512], P('isdf', None, 'band'), may hold values from -6 to 6
- cond_coef: bfloat16 [512, 8192], P('band', 'isdf'), may hold values from -0.25 to 0.25
- val_coef: bfloat16 [512, 8192], P('band', 'isdf'), may hold values from -1.5 to 1.5
- kernel: bfloat16 [8192, 8192], P('isdf', 'band'), may hold values from -0.09375 to 0.09375
- block_mask: int32 [64, 64], P('isdf', 'band'), may hold values from 0 to 1, as said below
Outputs:
- sigma: bfloat16 [512, 2, 512], P('isdf', None, 'band')
The draws below stay inside these ranges and needn't reach their ends.
Inputs may be any that keep to these rules, and one draw needn't show every extreme that they name: `block_mask`: 0 or 1; every block on the diagonal and within two blocks of it, cyclically, is 1.
All inputs are finite; a program needn't handle non-finite values.
Results may differ from the reference program's by a relative error of at most 0.0058.
Values may be sent and summed in bfloat16 or wider, within the bound.
A program may use at most 64 MiB of HBM per device.

```python
import jax
import jax.numpy as jnp
from jax import lax

MU_DEV = 1024
NT = 2
BLK = 128
NV = 512
NC = 512
NMU = 8192
NB = 64


def draw_block_mask(key, part):
    key = jax.random.fold_in(key, 7)
    level_key, pick_key = jax.random.split(key)
    levels = jax.random.randint(level_key, (NB,), 0, 4)
    picks = jax.random.randint(pick_key, (NB, NB), 0, 8)
    kept = picks < 2 * levels[:, None] + 1
    row_ids = jnp.arange(NB)[:, None]
    col_ids = jnp.arange(NB)[None, :]
    gap = jnp.abs(row_ids - col_ids)
    gap = jnp.minimum(gap, NB - gap)
    kept = jnp.logical_or(kept, gap <= 2)
    return jnp.where(kept, 1, 0).astype(jnp.int32)


def block_levels(rng, shape, cuts, low, largest):
    def one(dim, parts):
        draws = jax.random.uniform(jax.random.fold_in(jax.random.fold_in(rng, 6), dim), (parts,), jnp.float32, low / len(cuts), largest / len(cuts))
        return jnp.repeat(jnp.exp(draws), shape[dim] // parts).reshape((-1,) + (1,) * (len(shape) - dim - 1))

    gain = one(*cuts[0])
    for cut in cuts[1:]:
        gain = gain * one(*cut)
    return gain


def scatter_about(own_key, shape, scale, bound, pieces=(), kind=jnp.bfloat16):
    drawn = jax.random.normal(own_key, shape, jnp.float32) * scale
    if len(pieces) > 0:
        drawn = block_levels(own_key, shape, pieces, -0.22, 0.18) * drawn
    return jnp.clip(drawn, min=-bound, max=bound).astype(kind)


def setup_inputs(seed: int = 0) -> dict:
    streams_of = jax.random.split(jax.random.key(seed), 6)
    trial = scatter_about(streams_of[0], (NC, NT, NV), 1.0, 6.0, ((0, 8), (2, 4)))
    cond_coef = scatter_about(streams_of[1], (NC, NMU), NC ** -0.5, 0.25, ((0, 4), (1, 8)))
    val_coef = scatter_about(streams_of[2], (NV, NMU), ((NC / (NMU * NV)) ** 0.25), 1.5, ((0, 4), (1, 8)))
    kernel = scatter_about(streams_of[3], (NMU, NMU), (NMU // 2) ** -0.5, 0.09375, ((0, 8), (1, 4)))
    block_mask = draw_block_mask(jax.random.fold_in(streams_of[5], 71), 0)
    return dict(trial=trial, cond_coef=cond_coef, val_coef=val_coef, kernel=kernel, block_mask=block_mask)


def reference(trial, cond_coef, val_coef, kernel, block_mask):
    flat_trial = trial.reshape(NC, NT * NV)
    block_rows = MU_DEV // BLK

    def forward(screen_acc, index):
        offset = (index * MU_DEV).astype(jnp.int32)
        cond_block = lax.dynamic_slice_in_dim(cond_coef, offset, MU_DEV, 1)
        val_block = lax.dynamic_slice_in_dim(val_coef, offset, MU_DEV, 1)
        pairs = lax.dot_general(flat_trial, cond_block, (((0,), (0,)), ((), ())), preferred_element_type=jnp.float32)
        projected = jnp.sum(pairs.reshape(NT, NV, MU_DEV) * val_block.astype(jnp.float32)[None], axis=1)
        rounded = projected.astype(jnp.bfloat16)
        kernel_rows = lax.dynamic_slice_in_dim(kernel, offset, MU_DEV, 0)
        mask_part = lax.dynamic_slice_in_dim(block_mask, (index * block_rows).astype(jnp.int32), block_rows, 0)
        shaped = kernel_rows.reshape(block_rows, BLK, NB, BLK)
        masked = jnp.where(mask_part[:, None, :, None] > 0, shaped, jnp.zeros((), kernel.dtype)).reshape(MU_DEV, NMU)
        return screen_acc + jnp.dot(rounded, masked, preferred_element_type=jnp.float32), None

    screened, _ = lax.scan(forward, jnp.zeros((NT, NMU), jnp.float32), jnp.arange(NMU // MU_DEV))

    def backward(total, index):
        offset = (index * MU_DEV).astype(jnp.int32)
        cond_block = lax.dynamic_slice_in_dim(cond_coef, offset, MU_DEV, 1)
        val_block = lax.dynamic_slice_in_dim(val_coef, offset, MU_DEV, 1)
        screen_block = lax.dynamic_slice_in_dim(screened, offset, MU_DEV, 1)
        weighted = (val_block.astype(jnp.float32)[None] * screen_block[:, None, :]).astype(jnp.bfloat16)
        weighted = weighted.reshape(NT * NV, MU_DEV)
        return total + lax.dot_general(cond_block, weighted, (((1,), (1,)), ((), ())), preferred_element_type=jnp.float32), None

    summed, _ = lax.scan(backward, jnp.zeros((NC, NT * NV), jnp.float32), jnp.arange(NMU // MU_DEV))
    return summed.reshape(NC, NT, NV).astype(jnp.bfloat16)
```

```python
import functools

import jax
import jax.numpy as jnp
from jax import lax
from jax.experimental import pallas as pl
from jax.experimental.pallas import tpu as pltpu
from jax.sharding import PartitionSpec as P

F32 = jnp.float32
BF16 = jnp.bfloat16


def remote(src, dst, send_sem, recv_sem, band, isdf):
    return pltpu.make_async_remote_copy(
        src_ref=src,
        dst_ref=dst,
        send_sem=send_sem,
        recv_sem=recv_sem,
        device_id=(band, isdf),
        device_id_type=pl.DeviceIdType.MESH,
    )


def body(
    nb, n, nt, r, R,
    trial_ref, cond_ref, val_ref, kern_ref, mask_ref, out_ref,
    trial_my, trial_all, cond_all, val_all, kern_v, q_ref, proj_all, screen_my,
    screen_all, w_ref, red_my, red_all, mix, lsem,
    cond_s, cond_r, val_s, val_r, trial_s, trial_r, proj_s, proj_r,
    screen_s, screen_r, red_s, red_r,
):
    b = lax.axis_index("band")
    i = lax.axis_index("isdf")
    k = lax.rem(b, 2)
    g = b // 2
    ng = nb // 2
    rows, points = cond_ref.shape
    crow = rows // r
    vrow = val_ref.shape[0]
    npc = ng * r
    home = lax.rem(i // r, 2)
    slot = (i // (2 * r)) * r + lax.rem(i, r)
    mine = home == k

    def piece_isdf(p):
        return r * (2 * (p // r) + k) + p % r

    kern_cp = pltpu.make_async_copy(kern_ref, kern_v, lsem.at[0])
    own_cond = pltpu.make_async_copy(cond_ref, cond_all.at[g], lsem.at[1])
    own_val = pltpu.make_async_copy(
        val_ref, val_all.at[pl.ds(pl.multiple_of(k * vrow, vrow), vrow)], lsem.at[2])
    own_val.start()
    own_cond.start()
    kern_cp.start()

    barrier = pltpu.get_barrier_semaphore()

    def greet(bb, ii):
        pl.semaphore_signal(barrier, inc=1, device_id=(bb, ii),
                            device_id_type=pl.DeviceIdType.MESH)

    for d in range(1, nb):
        greet(lax.rem(b + d, nb), i)
    for p in range(npc):
        for c in range(2):
            ip = piece_isdf(p)
            @pl.when(jnp.logical_or(ip != i, k != c))
            def _():
                greet(2 * g + c, ip)
    for d in range(n):
        ii = lax.rem(i + d, n)
        sb = i // R
        if d == 0:
            @pl.when(sb != b)
            def _():
                greet(sb, ii)
            @pl.when(jnp.logical_not(mine))
            def _():
                greet(2 * g + home, ii)
        else:
            greet(sb, ii)
            greet(2 * g + home, ii)

    mix[...] = trial_ref[...].astype(F32)
    for t in range(nt):
        trial_my[t] = mix[pl.ds(t, crow, stride=nt), :].astype(BF16)
    vcols = pl.ds(pl.multiple_of(k * vrow, vrow), vrow)

    @pl.when(mine)
    def _():
        trial_all[slot, :, :, vcols] = trial_my[...]

    total = (nb - 1) + n + nb * R + npc * 2
    selfs = 2 * jnp.where(mine, 1, 0) + jnp.where(i // R == b, 1, 0)
    pl.semaphore_wait(barrier, total - selfs)

    conds = []
    for h in range(r):
        for d in range(1, ng):
            gg = lax.rem(g + d, ng)
            cp = remote(cond_ref.at[pl.ds(h * crow, crow)],
                        cond_all.at[g, pl.ds(h * crow, crow)],
                        cond_s.at[d, h], cond_r.at[g, h], 2 * gg + k, i)
            cp.start()
            conds.append(cp)
    trials = []
    for d in list(range(1, n)) + [0]:
        ii = lax.rem(i + d, n)
        cp = remote(trial_my, trial_all.at[slot, :, :, vcols],
                    trial_s.at[d], trial_r.at[slot, k], 2 * g + home, ii)
        trials.append(cp)
        if d == 0:
            pl.when(jnp.logical_not(mine))(cp.start)
        else:
            cp.start()
    val_cp = remote(val_ref, val_all.at[pl.ds(pl.multiple_of(k * vrow, vrow), vrow)],
                    val_s, val_r, 2 * g + (1 - k), i)
    val_cp.start()

    own_val.wait()
    val_cp.wait_recv()
    for p in range(npc):
        for c in range(2):
            @pl.when(jnp.logical_or(piece_isdf(p) != i, k != c))
            def _():
                remote(trial_my, trial_all.at[p, :, :, pl.ds(c * vrow, vrow)],
                       trial_s.at[0], trial_r.at[p, c], b, i).wait_recv()
        lhs = trial_all[p].reshape(nt * crow, 2 * vrow)
        q_ref[p] = jnp.dot(lhs, val_all[...], preferred_element_type=F32)

    width = 256
    acc = None
    own_cond.wait()
    proj_all[b] = jnp.zeros((nt, points), F32)
    for d in range(ng):
        gg = lax.rem(g + d, ng)
        for h in range(r):
            if d > 0:
                remote(cond_ref.at[pl.ds(h * crow, crow)],
                       cond_all.at[gg, pl.ds(h * crow, crow)],
                       cond_s.at[d, h], cond_r.at[gg, h], b, i).wait_recv()
            for j in range(points // width):
                cols = pl.ds(j * width, width)
                cb = cond_all[gg, pl.ds(h * crow, crow), cols].astype(F32)
                for t in range(nt):
                    x = q_ref[gg * r + h, pl.ds(t * crow, crow), cols] * cb
                    proj_all[b, pl.ds(t, 1), cols] += jnp.sum(x, axis=0, keepdims=True)

    projs = []
    for d in range(1, nb):
        bb = lax.rem(b + d, nb)
        cp = remote(proj_all.at[b], proj_all.at[b], proj_s.at[d], proj_r.at[b], bb, i)
        cp.start()
        projs.append(cp)

    mrows, mcols = mask_ref.shape
    blk = points // mrows
    cols_dev = kern_ref.shape[1]
    spread = (lax.broadcasted_iota(jnp.int32, (mcols, cols_dev), 1) // blk
              == lax.broadcasted_iota(jnp.int32, (mcols, cols_dev), 0))
    keep = jnp.dot((mask_ref[...] > 0).astype(F32).astype(BF16),
                   spread.astype(F32).astype(BF16), preferred_element_type=F32)
    here = (lax.broadcasted_iota(jnp.int32, (mrows, points), 1) // blk
            == lax.broadcasted_iota(jnp.int32, (mrows, points), 0))
    kern_cp.wait()

    for d in range(1, nb):
        bb = lax.rem(b + d, nb)
        remote(proj_all.at[bb], proj_all.at[bb], proj_s.at[d], proj_r.at[bb], b, i).wait_recv()
    proj = proj_all[0]
    for s in range(1, nb):
        proj = proj + proj_all[s]
    lhs = jnp.concatenate(
        [jnp.where(here, proj[t:t + 1], 0.0) for t in range(nt)], axis=0).astype(BF16)
    scr = jnp.dot(lhs, kern_v[...], preferred_element_type=F32)
    for t in range(nt):
        s = jnp.sum(scr[t * mrows:(t + 1) * mrows] * keep, axis=0, keepdims=True)
        for h in range(R):
            screen_my[h, pl.ds(t, 1), :] = s[:, h * points:(h + 1) * points]

    screens = []
    for h in range(R):
        ii = R * b + h
        for d in range(nb):
            bb = lax.rem(b + d, nb)
            cp = remote(screen_my.at[h], screen_all.at[i], screen_s.at[h, d],
                        screen_r.at[i], bb, ii)
            if d == 0:
                away = ii != i
                pl.when(away)(cp.start)

                @pl.when(jnp.logical_not(away))
                def _():
                    screen_all[i] = screen_my[h]
                screens.append((cp, away))
            else:
                cp.start()
                screens.append((cp, None))

    for d in range(n):
        ii = lax.rem(i + d, n)
        cp = remote(screen_my.at[0], screen_all.at[ii], screen_s.at[0, 0],
                    screen_r.at[ii], b, i)
        if d == 0:
            pl.when(i // R != b)(cp.wait_recv)
        else:
            cp.wait_recv()
    scr = screen_all[0]
    for s in range(1, n):
        scr = scr + screen_all[s]

    for t in range(nt):
        w_ref[pl.ds(t * 2 * vrow, 2 * vrow)] = (
            val_all[...].astype(F32) * scr[t:t + 1]).astype(BF16)
    reds = []
    for gg in range(ng):
        part = lax.dot_general(cond_all[gg], w_ref[...], (((1,), (1,)), ((), ())),
                               preferred_element_type=F32).astype(BF16)
        for h in range(r):
            p = gg * r + h
            ii = piece_isdf(p)
            for c in range(2):
                for t in range(nt):
                    lo = t * 2 * vrow + c * vrow
                    red_my[p, c, t] = part[h * crow:(h + 1) * crow, lo:lo + vrow]
                cp = remote(red_my.at[p, c], red_all.at[i], red_s.at[p, c],
                            red_r.at[i], 2 * g + c, ii)
                away = jnp.logical_or(ii != i, k != c)
                pl.when(away)(cp.start)

                @pl.when(jnp.logical_not(away))
                def _():
                    red_all[i] = red_my[p, c]
                reds.append((cp, away))

    for d in range(n):
        ii = lax.rem(i + d, n)
        cp = remote(red_my.at[0, 0], red_all.at[ii], red_s.at[0, 0], red_r.at[ii], b, i)
        if d == 0:
            pl.when(jnp.logical_not(mine))(cp.wait_recv)
        else:
            cp.wait_recv()
    for t in range(nt):
        tot = red_all[0, t].astype(F32)
        for s in range(1, n):
            tot = tot + red_all[s, t].astype(F32)
        mix[pl.ds(t, crow, stride=nt), :] = tot
    out_ref[...] = mix[...].astype(BF16)

    for cp in conds + projs + [val_cp]:
        cp.wait_send()
    for cp in trials[:-1]:
        cp.wait_send()
    pl.when(jnp.logical_not(mine))(trials[-1].wait_send)
    for cp, away in screens + reds:
        if away is None:
            cp.wait_send()
        else:
            pl.when(away)(cp.wait_send)


def on_device(nb, n, trial, cond_coef, val_coef, kernel, block_mask):
    crow, nt, vrow = trial.shape
    rows, points = cond_coef.shape
    r = rows // crow
    R = kernel.shape[1] // points
    ng = nb // 2
    npc = ng * r
    dma = pltpu.SemaphoreType.DMA
    anyspec = pl.BlockSpec(memory_space=pl.ANY)
    vspec = pl.BlockSpec(memory_space=pltpu.VMEM)
    out = pl.pallas_call(
        functools.partial(body, nb, n, nt, r, R),
        out_shape=jax.ShapeDtypeStruct((crow * nt, vrow), BF16),
        in_specs=[vspec, anyspec, anyspec, anyspec, vspec],
        out_specs=vspec,
        scratch_shapes=[
            pltpu.VMEM((nt, crow, vrow), BF16),
            pltpu.VMEM((npc, nt, crow, 2 * vrow), BF16),
            pltpu.VMEM((ng, rows, points), BF16),
            pltpu.VMEM((2 * vrow, points), BF16),
            pltpu.VMEM(kernel.shape, BF16),
            pltpu.VMEM((npc, nt * crow, points), F32),
            pltpu.VMEM((nb, nt, points), F32),
            pltpu.VMEM((R, nt, points), F32),
            pltpu.VMEM((n, nt, points), F32),
            pltpu.VMEM((nt * 2 * vrow, points), BF16),
            pltpu.VMEM((npc, 2, nt, crow, vrow), BF16),
            pltpu.VMEM((n, nt, crow, vrow), BF16),
            pltpu.VMEM((nt * crow, vrow), F32),
            dma((3,)),
            dma((ng, r)), dma((ng, r)),
            dma, dma,
            dma((n,)), dma((npc, 2)),
            dma((nb,)), dma((nb,)),
            dma((R, nb)), dma((n,)),
            dma((npc, 2)), dma((n,)),
        ],
        compiler_params=pltpu.CompilerParams(
            collective_id=0, has_side_effects=True, vmem_limit_bytes=50 * 1024 * 1024),
        name="sigma_product",
    )(trial.reshape(crow * nt, vrow), cond_coef, val_coef, kernel, block_mask)
    return out.reshape(trial.shape)


def solution(mesh):
    return jax.shard_map(
        functools.partial(on_device, mesh.shape["band"], mesh.shape["isdf"]),
        mesh=mesh,
        in_specs=(
            P("isdf", None, "band"),
            P("band", "isdf"),
            P("band", "isdf"),
            P("isdf", "band"),
            P("isdf", "band"),
        ),
        out_specs=P("isdf", None, "band"),
        check_vma=False,
    )
```

```python
import functools

import jax
import jax.numpy as jnp
from jax import lax
from jax.experimental import pallas as pl
from jax.experimental.pallas import tpu as pltpu
from jax.sharding import PartitionSpec as P

F32 = jnp.float32
BF16 = jnp.bfloat16


def remote(src, dst, send_sem, recv_sem, band, isdf):
    return pltpu.make_async_remote_copy(
        src_ref=src,
        dst_ref=dst,
        send_sem=send_sem,
        recv_sem=recv_sem,
        device_id=(band, isdf),
        device_id_type=pl.DeviceIdType.MESH,
    )


def body(
    nb, n, nt, r, R,
    trial_ref, cond_ref, val_ref, kern_ref, mask_ref, out_ref,
    trial_in, mask_in, trial_my, trial_all, cond_all, val_all, kern_v, q_ref, acc_ref, proj_all, screen_my,
    screen_all, w_ref, red_my, red_all, mix, lsem,
    cond_s, cond_r, val_s, val_r, trial_s, trial_r, proj_s, proj_r,
    screen_s, screen_r, red_s, red_r,
):
    b = lax.axis_index("band")
    i = lax.axis_index("isdf")
    k = lax.rem(b, 2)
    g = b // 2
    ng = nb // 2
    rows, points = cond_ref.shape
    crow = rows // r
    vrow = val_ref.shape[0]
    npc = ng * r
    home = lax.rem(i // r, 2)
    slot = (i // (2 * r)) * r + lax.rem(i, r)
    mine = home == k

    def piece_isdf(p):
        return r * (2 * (p // r) + k) + p % r

    barrier = pltpu.get_barrier_semaphore()

    def greet(bb, ii):
        pl.semaphore_signal(barrier, inc=1, device_id=(bb, ii),
                            device_id_type=pl.DeviceIdType.MESH)

    for p in range(npc):
        for c in range(2):
            ip = piece_isdf(p)
            @pl.when(ip != i)
            def _():
                greet(2 * g + c, ip)
    for d in range(1, nb):
        greet(lax.rem(b + d, nb), i)

    kern_cp = pltpu.make_async_copy(kern_ref, kern_v, lsem.at[0])
    own_cond = pltpu.make_async_copy(cond_ref, cond_all.at[g], lsem.at[1])
    own_val = pltpu.make_async_copy(
        val_ref, val_all.at[pl.ds(pl.multiple_of(k * vrow, vrow), vrow)], lsem.at[2])
    trial_cp = pltpu.make_async_copy(trial_ref, trial_in, lsem.at[3])
    mask_cp = pltpu.make_async_copy(mask_ref, mask_in, lsem.at[4])
    trial_cp.start()
    own_val.start()
    own_cond.start()
    mask_cp.start()
    kern_cp.start()

    trial_cp.wait()
    mix[...] = trial_in[...].astype(F32)
    for t in range(nt):
        trial_my[t] = mix[pl.ds(t, crow, stride=nt), :].astype(BF16)
    vcols = pl.ds(pl.multiple_of(k * vrow, vrow), vrow)

    @pl.when(mine)
    def _():
        trial_all[slot, :, :, vcols] = trial_my[...]

    pl.semaphore_wait(barrier, nb - 1 + n - 1)

    pending = []
    val_cp = remote(val_ref, val_all.at[pl.ds(pl.multiple_of(k * vrow, vrow), vrow)],
                    val_s, val_r, 2 * g + (1 - k), i)
    val_cp.start()
    pending.append(val_cp.wait_send)
    for h in range(r):
        for d in range(1, ng):
            gg = lax.rem(g + d, ng)
            cp = remote(cond_ref.at[pl.ds(h * crow, crow)],
                        cond_all.at[g, pl.ds(h * crow, crow)],
                        cond_s.at[d, h], cond_r.at[g, h], 2 * gg + k, i)
            cp.start()
            pending.append(cp.wait_send)
    for d in list(range(1, n)) + [0]:
        ii = lax.rem(i + d, n)
        cp = remote(trial_my, trial_all.at[slot, :, :, vcols],
                    trial_s.at[d], trial_r.at[slot, k], 2 * g + home, ii)
        if d == 0:
            pl.when(jnp.logical_not(mine))(cp.start)
            pending.append(functools.partial(pl.when(jnp.logical_not(mine)), cp.wait_send))
        else:
            cp.start()
            pending.append(cp.wait_send)

    own_val.wait()
    val_cp.wait_recv()
    for p in range(npc):
        for c in range(2):
            @pl.when(jnp.logical_or(piece_isdf(p) != i, k != c))
            def _():
                remote(trial_my, trial_all.at[p, :, :, pl.ds(c * vrow, vrow)],
                       trial_s.at[0], trial_r.at[p, c], b, i).wait_recv()
        if p % r == r - 1:
            lo = p - r + 1
            lhs = trial_all[lo:p + 1].reshape(r * nt * crow, 2 * vrow)
            q_ref[lo:p + 1] = jnp.dot(
                lhs, val_all[...], preferred_element_type=F32
            ).reshape(r, nt * crow, points)

    width = 256
    own_cond.wait()
    for d in range(ng):
        gg = lax.rem(g + d, ng)
        for h in range(r):
            if d > 0:
                remote(cond_ref.at[pl.ds(h * crow, crow)],
                       cond_all.at[gg, pl.ds(h * crow, crow)],
                       cond_s.at[d, h], cond_r.at[gg, h], b, i).wait_recv()
            for j in range(points // width):
                cols = pl.ds(j * width, width)
                cb = cond_all[gg, pl.ds(h * crow, crow), cols].astype(F32)
                for t in range(nt):
                    x = q_ref[gg * r + h, pl.ds(t * crow, crow), cols] * cb
                    x = jnp.sum(x.reshape(crow // 8, 8, width), axis=0)
                    if d == 0 and h == 0:
                        acc_ref[t, :, cols] = x
                    else:
                        acc_ref[t, :, cols] += x
    for t in range(nt):
        proj_all[b, pl.ds(t, 1), :] = jnp.sum(acc_ref[t], axis=0, keepdims=True)

    for d in range(1, nb):
        bb = lax.rem(b + d, nb)
        cp = remote(proj_all.at[b], proj_all.at[b], proj_s.at[d], proj_r.at[b], bb, i)
        cp.start()
        pending.append(cp.wait_send)

    mask_cp.wait()
    mrows, mcols = mask_ref.shape
    blk = points // mrows
    cols_dev = kern_ref.shape[1]
    spread = (lax.broadcasted_iota(jnp.int32, (mcols, cols_dev), 1) // blk
              == lax.broadcasted_iota(jnp.int32, (mcols, cols_dev), 0))
    keep = jnp.dot((mask_in[...] > 0).astype(F32).astype(BF16),
                   spread.astype(F32).astype(BF16), preferred_element_type=F32)
    here = (lax.broadcasted_iota(jnp.int32, (mrows, points), 1) // blk
            == lax.broadcasted_iota(jnp.int32, (mrows, points), 0))
    kern_cp.wait()

    for d in range(1, nb):
        bb = lax.rem(b + d, nb)
        remote(proj_all.at[bb], proj_all.at[bb], proj_s.at[d], proj_r.at[bb], b, i).wait_recv()
    proj = proj_all[0]
    for s in range(1, nb):
        proj = proj + proj_all[s]
    lhs = jnp.concatenate(
        [jnp.where(here, proj[t:t + 1], 0.0) for t in range(nt)], axis=0).astype(BF16)
    scr = jnp.dot(lhs, kern_v[...], preferred_element_type=F32)
    for t in range(nt):
        s = jnp.sum(scr[t * mrows:(t + 1) * mrows] * keep, axis=0, keepdims=True)
        for h in range(R):
            screen_my[h, pl.ds(t, 1), :] = s[:, h * points:(h + 1) * points]

    for h in range(R):
        ii = R * b + h
        for d in range(nb):
            bb = lax.rem(b + d, nb)
            cp = remote(screen_my.at[h], screen_all.at[i], screen_s.at[h, d],
                        screen_r.at[i], bb, ii)
            if d == 0:
                away = ii != i
                pl.when(away)(cp.start)

                @pl.when(jnp.logical_not(away))
                def _():
                    screen_all[i] = screen_my[h]
                pending.append(functools.partial(pl.when(away), cp.wait_send))
            else:
                cp.start()
                pending.append(cp.wait_send)

    for d in range(n):
        ii = lax.rem(i + d, n)
        cp = remote(screen_my.at[0], screen_all.at[ii], screen_s.at[0, 0],
                    screen_r.at[ii], b, i)
        if d == 0:
            pl.when(i // R != b)(cp.wait_recv)
        else:
            cp.wait_recv()
    scr = screen_all[0]
    for s in range(1, n):
        scr = scr + screen_all[s]

    for t in range(nt):
        w_ref[pl.ds(t * 2 * vrow, 2 * vrow)] = (
            val_all[...].astype(F32) * scr[t:t + 1]).astype(BF16)
    for gg in range(ng):
        part = lax.dot_general(cond_all[gg], w_ref[...], (((1,), (1,)), ((), ())),
                               preferred_element_type=F32).astype(BF16)
        for h in range(r):
            p = gg * r + h
            ii = piece_isdf(p)
            for c in range(2):
                for t in range(nt):
                    lo = t * 2 * vrow + c * vrow
                    red_my[p, c, t] = part[h * crow:(h + 1) * crow, lo:lo + vrow]
                cp = remote(red_my.at[p, c], red_all.at[i], red_s.at[p, c],
                            red_r.at[i], 2 * g + c, ii)
                away = jnp.logical_or(ii != i, k != c)
                pl.when(away)(cp.start)

                @pl.when(jnp.logical_not(away))
                def _():
                    red_all[i] = red_my[p, c]
                pending.append(functools.partial(pl.when(away), cp.wait_send))

    for d in range(n):
        ii = lax.rem(i + d, n)
        cp = remote(red_my.at[0, 0], red_all.at[ii], red_s.at[0, 0], red_r.at[ii], b, i)
        if d == 0:
            pl.when(jnp.logical_not(mine))(cp.wait_recv)
        else:
            cp.wait_recv()
    for t in range(nt):
        tot = red_all[0, t].astype(F32)
        for s in range(1, n):
            tot = tot + red_all[s, t].astype(F32)
        mix[pl.ds(t, crow, stride=nt), :] = tot
    out_ref[...] = mix[...].astype(BF16)

    for wait in pending:
        wait()


def on_device(nb, n, trial, cond_coef, val_coef, kernel, block_mask):
    crow, nt, vrow = trial.shape
    rows, points = cond_coef.shape
    r = rows // crow
    R = kernel.shape[1] // points
    ng = nb // 2
    npc = ng * r
    dma = pltpu.SemaphoreType.DMA
    hbm = pl.BlockSpec(memory_space=pltpu.HBM)
    vspec = pl.BlockSpec(memory_space=pltpu.VMEM)
    out = pl.pallas_call(
        functools.partial(body, nb, n, nt, r, R),
        out_shape=jax.ShapeDtypeStruct((crow * nt, vrow), BF16),
        in_specs=[hbm, hbm, hbm, hbm, hbm],
        out_specs=vspec,
        scratch_shapes=[
            pltpu.VMEM((crow * nt, vrow), BF16),
            pltpu.VMEM(block_mask.shape, jnp.int32),
            pltpu.VMEM((nt, crow, vrow), BF16),
            pltpu.VMEM((npc, nt, crow, 2 * vrow), BF16),
            pltpu.VMEM((ng, rows, points), BF16),
            pltpu.VMEM((2 * vrow, points), BF16),
            pltpu.VMEM(kernel.shape, BF16),
            pltpu.VMEM((npc, nt * crow, points), F32),
            pltpu.VMEM((nt, 8, points), F32),
            pltpu.VMEM((nb, nt, points), F32),
            pltpu.VMEM((R, nt, points), F32),
            pltpu.VMEM((n, nt, points), F32),
            pltpu.VMEM((nt * 2 * vrow, points), BF16),
            pltpu.VMEM((npc, 2, nt, crow, vrow), BF16),
            pltpu.VMEM((n, nt, crow, vrow), BF16),
            pltpu.VMEM((nt * crow, vrow), F32),
            dma((5,)),
            dma((ng, r)), dma((ng, r)),
            dma, dma,
            dma((n,)), dma((npc, 2)),
            dma((nb,)), dma((nb,)),
            dma((R, nb)), dma((n,)),
            dma((npc, 2)), dma((n,)),
        ],
        compiler_params=pltpu.CompilerParams(
            collective_id=0, has_side_effects=True, vmem_limit_bytes=63 * 1024 * 1024),
        name="sigma_product",
    )(trial.reshape(crow * nt, vrow), cond_coef, val_coef, kernel, block_mask)
    return out.reshape(trial.shape)


def solution(mesh):
    return jax.shard_map(
        functools.partial(on_device, mesh.shape["band"], mesh.shape["isdf"]),
        mesh=mesh,
        in_specs=(
            P("isdf", None, "band"),
            P("band", "isdf"),
            P("band", "isdf"),
            P("isdf", "band"),
            P("isdf", "band"),
        ),
        out_specs=P("isdf", None, "band"),
        check_vma=False,
    )
```

```python
import functools

import jax
import jax.numpy as jnp
from jax import lax
from jax.experimental import pallas as pl
from jax.experimental.pallas import tpu as pltpu
from jax.sharding import PartitionSpec as P

F32 = jnp.float32
BF16 = jnp.bfloat16


def remote(src, dst, send_sem, recv_sem, band, isdf):
    return pltpu.make_async_remote_copy(
        src_ref=src,
        dst_ref=dst,
        send_sem=send_sem,
        recv_sem=recv_sem,
        device_id=(band, isdf),
        device_id_type=pl.DeviceIdType.MESH,
    )


def body(
    nb, n, nt, r, R,
    trial_ref, cond_ref, val_ref, kern_ref, mask_ref, out_ref,
    trial_in, mask_in, trial_my, trial_all, cond_all, val_all, kern_v, q_ref, acc_ref, proj_all, screen_my,
    screen_all, w_ref, red_my, red_all, mix, lsem,
    cond_s, cond_r, val_s, val_r, trial_s, trial_r, proj_s, proj_r,
    screen_s, screen_r, red_s, red_r,
):
    b = lax.axis_index("band")
    i = lax.axis_index("isdf")
    k = lax.rem(b, 2)
    g = b // 2
    ng = nb // 2
    rows, points = cond_ref.shape
    crow = rows // r
    vrow = val_ref.shape[0]
    npc = ng * r
    home = lax.rem(i // r, 2)
    slot = (i // (2 * r)) * r + lax.rem(i, r)
    mine = home == k

    def piece_isdf(p):
        return r * (2 * (p // r) + k) + p % r

    barrier = pltpu.get_barrier_semaphore()

    def greet(bb, ii):
        pl.semaphore_signal(barrier, inc=1, device_id=(bb, ii),
                            device_id_type=pl.DeviceIdType.MESH)

    for p in range(npc):
        for c in range(2):
            ip = piece_isdf(p)
            @pl.when(ip != i)
            def _():
                greet(2 * g + c, ip)
    for d in range(1, nb):
        greet(lax.rem(b + d, nb), i)

    kern_cp = pltpu.make_async_copy(kern_ref, kern_v, lsem.at[0])
    own_cond = pltpu.make_async_copy(cond_ref, cond_all.at[g], lsem.at[1])
    own_val = pltpu.make_async_copy(
        val_ref, val_all.at[pl.ds(pl.multiple_of(k * vrow, vrow), vrow)], lsem.at[2])
    trial_cp = pltpu.make_async_copy(trial_ref, trial_in, lsem.at[3])
    mask_cp = pltpu.make_async_copy(mask_ref, mask_in, lsem.at[4])
    trial_cp.start()
    own_val.start()
    own_cond.start()
    mask_cp.start()
    kern_cp.start()

    trial_cp.wait()
    mix[...] = trial_in[...].astype(F32)
    for t in range(nt):
        trial_my[t] = mix[pl.ds(t, crow, stride=nt), :].astype(BF16)
    vcols = pl.ds(pl.multiple_of(k * vrow, vrow), vrow)

    @pl.when(mine)
    def _():
        trial_all[slot, :, :, vcols] = trial_my[...]

    pl.semaphore_wait(barrier, nb - 1 + n - 1)

    pending = []
    val_cp = remote(val_ref, val_all.at[pl.ds(pl.multiple_of(k * vrow, vrow), vrow)],
                    val_s, val_r, 2 * g + (1 - k), i)
    val_cp.start()
    pending.append(val_cp.wait_send)
    for h in range(r):
        for d in range(1, ng):
            gg = lax.rem(g + d, ng)
            cp = remote(cond_ref.at[pl.ds(h * crow, crow)],
                        cond_all.at[g, pl.ds(h * crow, crow)],
                        cond_s.at[d, h], cond_r.at[g, h], 2 * gg + k, i)
            cp.start()
            pending.append(cp.wait_send)
    for d in list(range(1, n)) + [0]:
        ii = lax.rem(i + d, n)
        cp = remote(trial_my, trial_all.at[slot, :, :, vcols],
                    trial_s.at[d], trial_r.at[slot, k], 2 * g + home, ii)
        if d == 0:
            pl.when(jnp.logical_not(mine))(cp.start)
            pending.append(functools.partial(pl.when(jnp.logical_not(mine)), cp.wait_send))
        else:
            cp.start()
            pending.append(cp.wait_send)

    own_val.wait()
    val_cp.wait_recv()
    for p in range(npc):
        for c in range(2):
            @pl.when(jnp.logical_or(piece_isdf(p) != i, k != c))
            def _():
                remote(trial_my, trial_all.at[p, :, :, pl.ds(c * vrow, vrow)],
                       trial_s.at[0], trial_r.at[p, c], b, i).wait_recv()
        if p % r == r - 1:
            lo = p - r + 1
            lhs = trial_all[lo:p + 1].reshape(r * nt * crow, 2 * vrow)
            q_ref[lo:p + 1] = jnp.dot(
                lhs, val_all[...], preferred_element_type=F32
            ).reshape(r, nt * crow, points)

    width = 256
    own_cond.wait()
    for d in range(ng):
        gg = lax.rem(g + d, ng)
        for h in range(r):
            if d > 0:
                remote(cond_ref.at[pl.ds(h * crow, crow)],
                       cond_all.at[gg, pl.ds(h * crow, crow)],
                       cond_s.at[d, h], cond_r.at[gg, h], b, i).wait_recv()
            for j in range(points // width):
                cols = pl.ds(j * width, width)
                cb = cond_all[gg, pl.ds(h * crow, crow), cols].astype(F32)
                for t in range(nt):
                    x = q_ref[gg * r + h, pl.ds(t * crow, crow), cols] * cb
                    x = jnp.sum(x.reshape(crow // 8, 8, width), axis=0)
                    if d == 0 and h == 0:
                        acc_ref[t, :, cols] = x
                    else:
                        acc_ref[t, :, cols] += x
    for t in range(nt):
        proj_all[b, pl.ds(t, 1), :] = jnp.sum(acc_ref[t], axis=0, keepdims=True)

    for d in range(1, nb):
        bb = lax.rem(b + d, nb)
        cp = remote(proj_all.at[b], proj_all.at[b], proj_s.at[d], proj_r.at[b], bb, i)
        cp.start()
        pending.append(cp.wait_send)

    mask_cp.wait()
    mrows, mcols = mask_ref.shape
    blk = points // mrows
    cols_dev = kern_ref.shape[1]
    spread = (lax.broadcasted_iota(jnp.int32, (mcols, cols_dev), 1) // blk
              == lax.broadcasted_iota(jnp.int32, (mcols, cols_dev), 0))
    keep = jnp.dot((mask_in[...] > 0).astype(F32).astype(BF16),
                   spread.astype(F32).astype(BF16), preferred_element_type=F32)
    here = (lax.broadcasted_iota(jnp.int32, (mrows, points), 1) // blk
            == lax.broadcasted_iota(jnp.int32, (mrows, points), 0))
    kern_cp.wait()

    for d in range(1, nb):
        bb = lax.rem(b + d, nb)
        remote(proj_all.at[bb], proj_all.at[bb], proj_s.at[d], proj_r.at[bb], b, i).wait_recv()
    proj = proj_all[0]
    for s in range(1, nb):
        proj = proj + proj_all[s]
    lhs = jnp.concatenate(
        [jnp.where(here, proj[t:t + 1], 0.0) for t in range(nt)], axis=0).astype(BF16)
    scr = jnp.dot(lhs, kern_v[...], preferred_element_type=F32)
    for t in range(nt):
        s = jnp.sum(scr[t * mrows:(t + 1) * mrows] * keep, axis=0, keepdims=True)
        for h in range(R):
            screen_my[h, pl.ds(t, 1), :] = s[:, h * points:(h + 1) * points]

    for e in list(range(1, ng)) + [0]:
        for h in range(R):
            ii = R * b + h
            for c in range(2):
                bb = 2 * lax.rem(g + e, ng) + lax.rem(k + 1 + c, 2)
                cp = remote(screen_my.at[h], screen_all.at[i], screen_s.at[h, 2 * e + c],
                            screen_r.at[i], bb, ii)
                if e == 0 and c == 1:
                    away = ii != i
                    pl.when(away)(cp.start)

                    @pl.when(jnp.logical_not(away))
                    def _():
                        screen_all[i] = screen_my[h]
                    pending.append(functools.partial(pl.when(away), cp.wait_send))
                else:
                    cp.start()
                    pending.append(cp.wait_send)

    for d in range(n):
        ii = lax.rem(i + d, n)
        cp = remote(screen_my.at[0], screen_all.at[ii], screen_s.at[0, 0],
                    screen_r.at[ii], b, i)
        if d == 0:
            pl.when(i // R != b)(cp.wait_recv)
        else:
            cp.wait_recv()
    scr = screen_all[0]
    for s in range(1, n):
        scr = scr + screen_all[s]

    for t in range(nt):
        w_ref[pl.ds(t * 2 * vrow, 2 * vrow)] = (
            val_all[...].astype(F32) * scr[t:t + 1]).astype(BF16)
    for e in range(ng):
        gg = lax.rem(i // (2 * r) + 1 + e, ng)
        part = lax.dot_general(cond_all[gg], w_ref[...], (((1,), (1,)), ((), ())),
                               preferred_element_type=F32).astype(BF16)
        for h in range(r):
            for c in range(2):
                for t in range(nt):
                    lo = t * 2 * vrow + c * vrow
                    red_my[gg * r + h, c, t] = part[h * crow:(h + 1) * crow, lo:lo + vrow]
        for q in range(r):
            h = lax.rem(i + 1 + q, r)
            p = gg * r + h
            ii = r * (2 * gg + k) + h
            for c in range(2):
                cp = remote(red_my.at[p, c], red_all.at[i], red_s.at[p, c],
                            red_r.at[i], 2 * g + c, ii)
                away = jnp.logical_or(ii != i, k != c)
                pl.when(away)(cp.start)

                @pl.when(jnp.logical_not(away))
                def _():
                    red_all[i] = red_my[p, c]
                pending.append(functools.partial(pl.when(away), cp.wait_send))

    for d in range(n):
        ii = lax.rem(i + d, n)
        cp = remote(red_my.at[0, 0], red_all.at[ii], red_s.at[0, 0], red_r.at[ii], b, i)
        if d == 0:
            pl.when(jnp.logical_not(mine))(cp.wait_recv)
        else:
            cp.wait_recv()
    for t in range(nt):
        tot = red_all[0, t].astype(F32)
        for s in range(1, n):
            tot = tot + red_all[s, t].astype(F32)
        mix[pl.ds(t, crow, stride=nt), :] = tot
    out_ref[...] = mix[...].astype(BF16)

    for wait in pending:
        wait()


def on_device(nb, n, trial, cond_coef, val_coef, kernel, block_mask):
    crow, nt, vrow = trial.shape
    rows, points = cond_coef.shape
    r = rows // crow
    R = kernel.shape[1] // points
    ng = nb // 2
    npc = ng * r
    dma = pltpu.SemaphoreType.DMA
    hbm = pl.BlockSpec(memory_space=pltpu.HBM)
    vspec = pl.BlockSpec(memory_space=pltpu.VMEM)
    out = pl.pallas_call(
        functools.partial(body, nb, n, nt, r, R),
        out_shape=pltpu.VMEM((crow * nt, vrow), BF16),
        in_specs=[hbm, hbm, hbm, hbm, hbm],
        out_specs=vspec,
        scratch_shapes=[
            pltpu.VMEM((crow * nt, vrow), BF16),
            pltpu.VMEM(block_mask.shape, jnp.int32),
            pltpu.VMEM((nt, crow, vrow), BF16),
            pltpu.VMEM((npc, nt, crow, 2 * vrow), BF16),
            pltpu.VMEM((ng, rows, points), BF16),
            pltpu.VMEM((2 * vrow, points), BF16),
            pltpu.VMEM(kernel.shape, BF16),
            pltpu.VMEM((npc, nt * crow, points), F32),
            pltpu.VMEM((nt, 8, points), F32),
            pltpu.VMEM((nb, nt, points), F32),
            pltpu.VMEM((R, nt, points), F32),
            pltpu.VMEM((n, nt, points), F32),
            pltpu.VMEM((nt * 2 * vrow, points), BF16),
            pltpu.VMEM((npc, 2, nt, crow, vrow), BF16),
            pltpu.VMEM((n, nt, crow, vrow), BF16),
            pltpu.VMEM((nt * crow, vrow), F32),
            dma((5,)),
            dma((ng, r)), dma((ng, r)),
            dma, dma,
            dma((n,)), dma((npc, 2)),
            dma((nb,)), dma((nb,)),
            dma((R, nb)), dma((n,)),
            dma((npc, 2)), dma((n,)),
        ],
        compiler_params=pltpu.CompilerParams(
            collective_id=0, has_side_effects=True, vmem_limit_bytes=63 * 1024 * 1024),
        name="sigma_product",
    )(trial.reshape(crow * nt, vrow), cond_coef, val_coef, kernel, block_mask)
    return out.reshape(trial.shape)


def solution(mesh):
    return jax.shard_map(
        functools.partial(on_device, mesh.shape["band"], mesh.shape["isdf"]),
        mesh=mesh,
        in_specs=(
            P("isdf", None, "band"),
            P("band", "isdf"),
            P("band", "isdf"),
            P("isdf", "band"),
            P("isdf", "band"),
        ),
        out_specs=P("isdf", None, "band"),
        check_vma=False,
    )
```

```python
import functools

import jax
import jax.numpy as jnp
from jax import lax
from jax.experimental import pallas as pl
from jax.experimental.pallas import tpu as pltpu
from jax.sharding import PartitionSpec as P

F32 = jnp.float32
BF16 = jnp.bfloat16


def remote(src, dst, send_sem, recv_sem, band, isdf):
    return pltpu.make_async_remote_copy(
        src_ref=src,
        dst_ref=dst,
        send_sem=send_sem,
        recv_sem=recv_sem,
        device_id=(band, isdf),
        device_id_type=pl.DeviceIdType.MESH,
    )


def body(
    nb, n, nt, r, R,
    trial_ref, cond_ref, val_ref, kern_ref, mask_ref, out_ref,
    trial_in, mask_in, trial_my, trial_all, cond_all, val_all, kern_v, q_ref, acc_ref, proj_all, screen_my,
    screen_all, w_ref, red_my, red_all, mix, lsem,
    cond_s, cond_r, val_s, val_r, trial_s, trial_r, proj_s, proj_r,
    screen_s, screen_r, red_s, red_r,
):
    b = lax.axis_index("band")
    i = lax.axis_index("isdf")
    k = lax.rem(b, 2)
    g = b // 2
    ng = nb // 2
    rows, points = cond_ref.shape
    crow = rows // r
    vrow = val_ref.shape[0]
    npc = ng * r
    home = lax.rem(i // r, 2)
    slot = (i // (2 * r)) * r + lax.rem(i, r)
    mine = home == k

    def piece_isdf(p):
        return r * (2 * (p // r) + k) + p % r

    barrier = pltpu.get_barrier_semaphore()

    def greet(bb, ii):
        pl.semaphore_signal(barrier, inc=1, device_id=(bb, ii),
                            device_id_type=pl.DeviceIdType.MESH)

    for p in range(npc):
        for c in range(2):
            ip = piece_isdf(p)
            @pl.when(ip != i)
            def _():
                greet(2 * g + c, ip)
    for d in range(1, nb):
        greet(lax.rem(b + d, nb), i)

    kern_cp = pltpu.make_async_copy(kern_ref, kern_v, lsem.at[0])
    own_cond = pltpu.make_async_copy(cond_ref, cond_all.at[g], lsem.at[1])
    own_val = pltpu.make_async_copy(
        val_ref, val_all.at[pl.ds(pl.multiple_of(k * vrow, vrow), vrow)], lsem.at[2])
    trial_cp = pltpu.make_async_copy(trial_ref, trial_in, lsem.at[3])
    mask_cp = pltpu.make_async_copy(mask_ref, mask_in, lsem.at[4])
    trial_cp.start()
    own_val.start()
    own_cond.start()
    mask_cp.start()
    kern_cp.start()

    trial_cp.wait()
    mix[...] = trial_in[...].astype(F32)
    for t in range(nt):
        trial_my[t] = mix[pl.ds(t, crow, stride=nt), :].astype(BF16)
    vcols = pl.ds(pl.multiple_of(k * vrow, vrow), vrow)

    @pl.when(mine)
    def _():
        trial_all[slot, :, :, vcols] = trial_my[...]

    pl.semaphore_wait(barrier, nb - 1 + n - 1)

    pending = []
    for h in range(r):
        for d in range(1, ng):
            gg = lax.rem(g + d, ng)
            cp = remote(cond_ref.at[pl.ds(h * crow, crow)],
                        cond_all.at[g, pl.ds(h * crow, crow)],
                        cond_s.at[d, h], cond_r.at[g, h], 2 * gg + k, i)
            cp.start()
            pending.append(cp.wait_send)
    val_cp = remote(val_ref, val_all.at[pl.ds(pl.multiple_of(k * vrow, vrow), vrow)],
                    val_s, val_r, 2 * g + (1 - k), i)
    val_cp.start()
    pending.append(val_cp.wait_send)
    for d in list(range(1, n)) + [0]:
        ii = lax.rem(i + d, n)
        cp = remote(trial_my, trial_all.at[slot, :, :, vcols],
                    trial_s.at[d], trial_r.at[slot, k], 2 * g + home, ii)
        if d == 0:
            pl.when(jnp.logical_not(mine))(cp.start)
            pending.append(functools.partial(pl.when(jnp.logical_not(mine)), cp.wait_send))
        else:
            cp.start()
            pending.append(cp.wait_send)

    own_val.wait()
    val_cp.wait_recv()
    for p in range(npc):
        for c in range(2):
            @pl.when(jnp.logical_or(piece_isdf(p) != i, k != c))
            def _():
                remote(trial_my, trial_all.at[p, :, :, pl.ds(c * vrow, vrow)],
                       trial_s.at[0], trial_r.at[p, c], b, i).wait_recv()
        if p % r == r - 1:
            lo = p - r + 1
            lhs = trial_all[lo:p + 1].reshape(r * nt * crow, 2 * vrow)
            q_ref[lo:p + 1] = jnp.dot(
                lhs, val_all[...], preferred_element_type=F32
            ).reshape(r, nt * crow, points)

    width = 256
    own_cond.wait()
    for d in range(ng):
        gg = lax.rem(g + d, ng)
        for h in range(r):
            if d > 0:
                remote(cond_ref.at[pl.ds(h * crow, crow)],
                       cond_all.at[gg, pl.ds(h * crow, crow)],
                       cond_s.at[d, h], cond_r.at[gg, h], b, i).wait_recv()
            for j in range(points // width):
                cols = pl.ds(j * width, width)
                cb = cond_all[gg, pl.ds(h * crow, crow), cols].astype(F32)
                for t in range(nt):
                    x = q_ref[gg * r + h, pl.ds(t * crow, crow), cols] * cb
                    x = jnp.sum(x.reshape(crow // 8, 8, width), axis=0)
                    if d == 0 and h == 0:
                        acc_ref[t, :, cols] = x
                    else:
                        acc_ref[t, :, cols] += x
    for t in range(nt):
        proj_all[b, pl.ds(t, 1), :] = jnp.sum(acc_ref[t], axis=0, keepdims=True)

    for d in list(range(2, nb)) + [1]:
        bb = 2 * lax.rem(g + d // 2, ng) + lax.rem(k + d, 2)
        cp = remote(proj_all.at[b], proj_all.at[b], proj_s.at[d], proj_r.at[b], bb, i)
        cp.start()
        pending.append(cp.wait_send)

    for wait in pending[:-(nb - 1)]:
        wait()
    del pending[:-(nb - 1)]

    mask_cp.wait()
    mrows, mcols = mask_ref.shape
    blk = points // mrows
    cols_dev = kern_ref.shape[1]
    spread = (lax.broadcasted_iota(jnp.int32, (mcols, cols_dev), 1) // blk
              == lax.broadcasted_iota(jnp.int32, (mcols, cols_dev), 0))
    keep = jnp.dot((mask_in[...] > 0).astype(F32).astype(BF16),
                   spread.astype(F32).astype(BF16), preferred_element_type=F32)
    here = (lax.broadcasted_iota(jnp.int32, (mrows, points), 1) // blk
            == lax.broadcasted_iota(jnp.int32, (mrows, points), 0))
    kern_cp.wait()

    for d in range(1, nb):
        bb = lax.rem(b + d, nb)
        remote(proj_all.at[bb], proj_all.at[bb], proj_s.at[d], proj_r.at[bb], b, i).wait_recv()
    proj = proj_all[0]
    for s in range(1, nb):
        proj = proj + proj_all[s]
    lhs = jnp.concatenate(
        [jnp.where(here, proj[t:t + 1], 0.0) for t in range(nt)], axis=0).astype(BF16)
    scr = jnp.dot(lhs, kern_v[...], preferred_element_type=F32)
    for t in range(nt):
        s = jnp.sum(scr[t * mrows:(t + 1) * mrows] * keep, axis=0, keepdims=True)
        for h in range(R):
            screen_my[h, pl.ds(t, 1), :] = s[:, h * points:(h + 1) * points]

    for e in list(range(1, ng)) + [0]:
        for h in range(R):
            ii = R * b + h
            for c in range(2):
                bb = 2 * lax.rem(g + e, ng) + lax.rem(k + 1 + c, 2)
                cp = remote(screen_my.at[h], screen_all.at[i], screen_s.at[h, 2 * e + c],
                            screen_r.at[i], bb, ii)
                if e == 0 and c == 1:
                    away = ii != i
                    pl.when(away)(cp.start)

                    @pl.when(jnp.logical_not(away))
                    def _():
                        screen_all[i] = screen_my[h]
                    pending.append(functools.partial(pl.when(away), cp.wait_send))
                else:
                    cp.start()
                    pending.append(cp.wait_send)

    for d in range(n):
        ii = lax.rem(i + d, n)
        cp = remote(screen_my.at[0], screen_all.at[ii], screen_s.at[0, 0],
                    screen_r.at[ii], b, i)
        if d == 0:
            pl.when(i // R != b)(cp.wait_recv)
        else:
            cp.wait_recv()
    scr = screen_all[0]
    for s in range(1, n):
        scr = scr + screen_all[s]

    for t in range(nt):
        w_ref[pl.ds(t * 2 * vrow, 2 * vrow)] = (
            val_all[...].astype(F32) * scr[t:t + 1]).astype(BF16)
    part = lax.dot_general(cond_all[...].reshape(ng * rows, points), w_ref[...],
                           (((1,), (1,)), ((), ())), preferred_element_type=F32).astype(BF16)
    for p in range(npc):
        for c in range(2):
            for t in range(nt):
                lo = t * 2 * vrow + c * vrow
                red_my[p, c, t] = part[p * crow:(p + 1) * crow, lo:lo + vrow]
    for e in range(ng):
        gg = lax.rem(i // (2 * r) + 1 + e, ng)
        for q in range(r):
            h = lax.rem(i + 1 + q, r)
            p = gg * r + h
            ii = r * (2 * gg + k) + h
            for c in range(2):
                cp = remote(red_my.at[p, c], red_all.at[i], red_s.at[p, c],
                            red_r.at[i], 2 * g + c, ii)
                away = jnp.logical_or(ii != i, k != c)
                pl.when(away)(cp.start)

                @pl.when(jnp.logical_not(away))
                def _():
                    red_all[i] = red_my[p, c]
                pending.append(functools.partial(pl.when(away), cp.wait_send))

    for wait in pending:
        wait()
    pending.clear()
    for d in range(n):
        ii = lax.rem(i + d, n)
        cp = remote(red_my.at[0, 0], red_all.at[ii], red_s.at[0, 0], red_r.at[ii], b, i)
        if d == 0:
            pl.when(jnp.logical_not(mine))(cp.wait_recv)
        else:
            cp.wait_recv()
    for t in range(nt):
        tot = red_all[0, t].astype(F32)
        for s in range(1, n):
            tot = tot + red_all[s, t].astype(F32)
        mix[pl.ds(t, crow, stride=nt), :] = tot
    out_ref[...] = mix[...].astype(BF16)


def on_device(nb, n, trial, cond_coef, val_coef, kernel, block_mask):
    crow, nt, vrow = trial.shape
    rows, points = cond_coef.shape
    r = rows // crow
    R = kernel.shape[1] // points
    ng = nb // 2
    npc = ng * r
    dma = pltpu.SemaphoreType.DMA
    hbm = pl.BlockSpec(memory_space=pltpu.HBM)
    vspec = pl.BlockSpec(memory_space=pltpu.VMEM)
    out = pl.pallas_call(
        functools.partial(body, nb, n, nt, r, R),
        out_shape=pltpu.VMEM((crow * nt, vrow), BF16),
        in_specs=[hbm, hbm, hbm, hbm, hbm],
        out_specs=vspec,
        scratch_shapes=[
            pltpu.VMEM((crow * nt, vrow), BF16),
            pltpu.VMEM(block_mask.shape, jnp.int32),
            pltpu.VMEM((nt, crow, vrow), BF16),
            pltpu.VMEM((npc, nt, crow, 2 * vrow), BF16),
            pltpu.VMEM((ng, rows, points), BF16),
            pltpu.VMEM((2 * vrow, points), BF16),
            pltpu.VMEM(kernel.shape, BF16),
            pltpu.VMEM((npc, nt * crow, points), F32),
            pltpu.VMEM((nt, 8, points), F32),
            pltpu.VMEM((nb, nt, points), F32),
            pltpu.VMEM((R, nt, points), F32),
            pltpu.VMEM((n, nt, points), F32),
            pltpu.VMEM((nt * 2 * vrow, points), BF16),
            pltpu.VMEM((npc, 2, nt, crow, vrow), BF16),
            pltpu.VMEM((n, nt, crow, vrow), BF16),
            pltpu.VMEM((nt * crow, vrow), F32),
            dma((5,)),
            dma((ng, r)), dma((ng, r)),
            dma, dma,
            dma((n,)), dma((npc, 2)),
            dma((nb,)), dma((nb,)),
            dma((R, nb)), dma((n,)),
            dma((npc, 2)), dma((n,)),
        ],
        compiler_params=pltpu.CompilerParams(
            collective_id=0, has_side_effects=True, vmem_limit_bytes=63 * 1024 * 1024),
        name="sigma_product",
    )(trial.reshape(crow * nt, vrow), cond_coef, val_coef, kernel, block_mask)
    return out.reshape(trial.shape)


def solution(mesh):
    return jax.shard_map(
        functools.partial(on_device, mesh.shape["band"], mesh.shape["isdf"]),
        mesh=mesh,
        in_specs=(
            P("isdf", None, "band"),
            P("band", "isdf"),
            P("band", "isdf"),
            P("isdf", "band"),
            P("isdf", "band"),
        ),
        out_specs=P("isdf", None, "band"),
        check_vma=False,
    )
```
